1024 devices in a mesh: sec: 64 (over z, core), op: 16 (over x, y).
Axes of the slice: x: 4, y: 4, z: 32, core: 2. Of those that a mesh axis runs over, the one named last changes fastest.
Arguments:
- psi: bfloat16 [3, 512, 8, 4096], P(None, 'sec'), may hold values from -23 to 23
- left_ops: bfloat16 [64, 512, 64, 64], P('op', 'sec'), may hold values from -4 to 4
- right_ops: bfloat16 [64, 512, 64, 64], P('op', 'sec'), may hold values from -4 to 4
- dest_dev: int32 [512, 8], replicated, may hold values from 0 to 63, as said below
- right_sub: int32 [512, 8], replicated, may hold values from 0 to 7
Outputs:
- sigma: bfloat16 [3, 512, 8, 4096], P(None, 'sec', None, 'op')
- subspace: float32 [3, 3], replicated
The draws below stay inside these ranges and needn't reach their ends.
Inputs may be any that keep to these rules, and one draw needn't show every extreme that they name: `dest_dev`: the 8 entries of a row differ. Rows come in runs of 8, one run for each index of sec; within one run no value appears more than 1 times, and some value appears exactly 1 times in every run.
All inputs are finite; a program needn't handle non-finite values.
Results may differ from the reference program's by a relative error of at most 0.017.
Values may be sent and summed in bfloat16 or wider, within the bound.
A program may use at most 64 MiB of HBM per device.

```python
import math
import jax
import jax.numpy as jnp
from jax import lax

B = 64
SEC_DEV = 8
PAIRS = 8
TERMS_DEV = 4
NVEC = 3
SEC = 512
TERMS = 64
N_SEC = 64
N_OP = 16


def operator_tiles(key, rising):
    first, second, third = jax.random.split(key, 3)
    noise = jax.random.truncated_normal(first, -4.0, 4.0, (TERMS, SEC, B, B))
    signs = jnp.where(jax.random.bernoulli(second, 0.5, (TERMS, SEC, 1, 1)), 1.0, -1.0)
    sizes = jax.random.uniform(third, (TERMS, SEC, 1, 1), minval=0.5, maxval=2.0)
    ident = jnp.eye(B, dtype=jnp.float32)
    scale = rising ** (jnp.arange(TERMS, dtype=jnp.float32) / TERMS - 0.5)
    tiles = (signs * sizes * ident + noise / math.sqrt(B)) * scale.reshape(TERMS, 1, 1, 1)
    return (tiles / math.sqrt(math.sqrt(TERMS))).astype(jnp.bfloat16)


def draw_left_ops(key, part):
    key = jax.random.fold_in(key, 21)
    return operator_tiles(key, 3.0)


def draw_right_ops(key, part):
    key = jax.random.fold_in(key, 22)
    return operator_tiles(key, 1.0)


def draw_psi(key, part):
    key = jax.random.fold_in(key, 31)
    first, second = jax.random.split(key, 2)
    rows = 10.0 ** (jax.random.uniform(second, (1, SEC, PAIRS, B, 1)) - 0.5)
    rise = 3.0 ** (jnp.arange(SEC, dtype=jnp.float32) / SEC - 0.5)
    base = jax.random.truncated_normal(first, -4.0, 4.0, (NVEC, SEC, PAIRS, B, B))
    values = base * rows * rise.reshape(1, SEC, 1, 1, 1)
    return values.reshape(NVEC, SEC, PAIRS, B * B).astype(jnp.bfloat16)


def draw_dest_dev(key, part):
    key = jax.random.fold_in(key, 11)
    key_hub, key_pos, key_perm = jax.random.split(key, 3)
    blocks_each = SEC_DEV * PAIRS
    reach = min(blocks_each, N_SEC)
    hub = jax.random.randint(key_hub, (), 0, N_SEC)
    where_zero = jax.random.randint(key_pos, (N_SEC, 1), 0, reach)
    perm_keys = jax.random.split(key_perm, N_SEC)
    perms = jax.vmap(lambda single: jax.random.permutation(single, N_SEC - 1))(perm_keys)
    column = jnp.arange(N_SEC, dtype=jnp.int32)[None, :]
    moved = jnp.clip(column - (column > where_zero).astype(jnp.int32), 0, N_SEC - 2)
    offsets = jnp.where(column == where_zero, 0, 1 + jnp.take_along_axis(perms, moved, axis=1))
    position = jnp.arange(blocks_each, dtype=jnp.int32) % N_SEC
    target = (hub + offsets[:, position]) % N_SEC
    return target.reshape(N_SEC * SEC_DEV, PAIRS).astype(jnp.int32)


def with_ends(result, own_key, smallest, largest):
    dims = result.shape
    index_at = [jax.random.randint(jax.random.fold_in(own_key, axis), (), 0, dims[axis]) for axis in range(len(dims))]
    result = result.at[tuple(index_at)].set(smallest)
    longest = dims.index(max(dims))
    index_at[longest] = (index_at[longest] + 1) % dims[longest]
    return result.at[tuple(index_at)].set(largest)


def setup_inputs(seed: int = 0) -> dict:
    splits = jax.random.split(jax.random.key(seed), 6)
    psi = draw_psi(jax.random.fold_in(splits[5], 71), 0)
    left_ops = draw_left_ops(jax.random.fold_in(splits[5], 71), 0)
    right_ops = draw_right_ops(jax.random.fold_in(splits[5], 71), 0)
    dest_dev = draw_dest_dev(jax.random.fold_in(splits[5], 71), 0)
    right_sub = with_ends(jax.random.randint(splits[4], (SEC, PAIRS), 0, SEC_DEV), jax.random.fold_in(splits[4], 1), 0, SEC_DEV - 1).astype(jnp.int32)
    return {"psi": psi, "left_ops": left_ops, "right_ops": right_ops, "dest_dev": dest_dev, "right_sub": right_sub}


def reference(psi, left_ops, right_ops, dest_dev, right_sub):
    right_sector = (dest_dev * SEC_DEV + right_sub).astype(jnp.int32)
    blocks = psi.reshape(NVEC, SEC, PAIRS, B, B).astype(jnp.float32)
    left_groups = left_ops.reshape(N_OP, TERMS_DEV, SEC, B, B)
    right_groups = right_ops.reshape(N_OP, TERMS_DEV, SEC, B, B)

    def one_group(carry, operators):
        left_set, right_set = operators
        partial_value = jnp.zeros((NVEC, SEC, PAIRS, B, B), jnp.float32)
        for term in range(TERMS_DEV):
            chosen = right_set[term][right_sector].astype(jnp.float32)
            inner = jnp.einsum('vspik,spjk->vspij', blocks, chosen).astype(jnp.bfloat16)
            partial_value = partial_value + jnp.einsum('sik,vspkj->vspij', left_set[term].astype(jnp.float32), inner.astype(jnp.float32))
        rounded = lax.optimization_barrier(partial_value.astype(jnp.bfloat16)).astype(jnp.float32)
        return carry + rounded, None

    start = jnp.zeros((NVEC, SEC, PAIRS, B, B), jnp.float32)
    total, _ = lax.scan(one_group, start, (left_groups, right_groups))
    total = total.reshape(NVEC, SEC, PAIRS, B * B)
    sigma = total.astype(jnp.bfloat16)
    subspace = jnp.einsum('vspx,wspx->vw', psi.astype(jnp.float32), total) / (SEC * PAIRS * B * B)
    return sigma, subspace
```

```python
import functools

import jax
import jax.numpy as jnp
from jax import lax
from jax.experimental import pallas as pl
from jax.experimental.pallas import tpu as pltpu
from jax.sharding import PartitionSpec as P

MESH = pl.DeviceIdType.MESH
CHUNKS = 2
F32 = jnp.float32
BF16 = jnp.bfloat16


def kernel(
    chips, groups, scale,
    tab_ref, idx_ref, psi_ref, left_ref, right_ref,
    sig_ref, sub_ref,
    ring, blk, pass_on, wide, lefts, stage, outbox, inbox, total, acc,
    dots, dots_op, dots_core, dots_chip, one, two, three, shelf,
    ring_send, ring_recv, pair_send, pair_recv, op_send, op_recv, dot_send, dot_recv,
):
    half = chips // 2
    vectors, secs, pairs, cells = psi_ref.shape
    batches = chips // 4
    per = secs // CHUNKS
    me = lax.axis_index("sec")
    core = lax.rem(me, 2)
    z = lax.div(me, 2)
    op = lax.axis_index("op")
    mate = z * 2 + 1 - core

    def chip(step):
        return lax.rem(z + step + chips, chips) * 2 + core

    def op_peer(step):
        return lax.rem(op + step, groups)

    barrier = pltpu.get_barrier_semaphore()

    def greet_chip(step, carry):
        pl.semaphore_signal(barrier, inc=1, device_id={"sec": chip(step)}, device_id_type=MESH)
        return carry

    def greet_op(step, carry):
        pl.semaphore_signal(barrier, inc=1, device_id={"op": op_peer(step)}, device_id_type=MESH)
        return carry

    lax.fori_loop(1, chips, greet_chip, 0)
    if groups > 1:
        lax.fori_loop(1, groups, greet_op, 0)
    pl.semaphore_signal(barrier, inc=1, device_id={"sec": mate}, device_id_type=MESH)

    def pack_right(s, carry):
        for high in range(2):
            ring[0, s, high * 64:(high + 1) * 64, :] = jnp.concatenate(
                [right_ref[2 * high, s], right_ref[2 * high + 1, s]], axis=1
            )
        return carry

    lax.fori_loop(0, secs, pack_right, 0)
    pl.semaphore_wait(barrier, chips + groups - 1)

    def ring_copy(way, hop, q):
        if way == 0:
            src, dst, target = hop - 1, hop, chip(1)
        else:
            src, dst, target = lax.rem(chips + 1 - hop, chips), chips - hop, chip(-1)
        return pltpu.make_async_remote_copy(
            src_ref=ring.at[src, pl.ds(q * per, per)],
            dst_ref=ring.at[dst, pl.ds(q * per, per)],
            send_sem=ring_send.at[way, hop, q],
            recv_sem=ring_recv.at[way, hop, q],
            device_id={"sec": target},
            device_id_type=MESH,
        )

    def last_way(q):
        return 0 if q < CHUNKS // 2 else 1

    for q in range(CHUNKS):
        ring_copy(0, 1, q).start()
        ring_copy(1, 1, q).start()

    def pair_copy(slot):
        return pltpu.make_async_remote_copy(
            src_ref=pass_on.at[slot],
            dst_ref=blk.at[chips + slot],
            send_sem=pair_send.at[slot],
            recv_sem=pair_recv.at[slot],
            device_id={"sec": mate},
            device_id_type=MESH,
        )

    def choose(slot):
        for s in range(secs):
            shelf[s] = ring[slot, s]
        pass_on[slot] = shelf[tab_ref[2, chips + slot]]
        pair_copy(slot).start()
        blk[slot] = shelf[tab_ref[2, slot]]

    choose(0)

    low = lax.broadcasted_iota(jnp.int32, (pairs, 128), 1) < 64

    def widen(step, carry):
        v = lax.div(step, secs)
        l = lax.rem(step, secs)
        for t in range(cells // 128):
            x = psi_ref[v, l, :, t * 128:(t + 1) * 128].astype(F32)
            r = pltpu.roll(x, 64, 1)
            wide[v, l, pl.ds(2 * t, pairs, stride=64), :] = jnp.where(low, x, r)
            wide[v, l, pl.ds(2 * t + 1, pairs, stride=64), :] = jnp.where(low, r, x)
        return carry

    lax.fori_loop(0, vectors * secs, widen, 0)

    def pack_left(l, carry):
        for high in range(2):
            lefts[l, high * 64:(high + 1) * 64, :] = jnp.concatenate(
                [left_ref[2 * high, l], left_ref[2 * high + 1, l]], axis=1
            )
        return carry

    lax.fori_loop(0, secs, pack_left, 0)
    acc[...] = jnp.zeros_like(acc)
    low64 = lax.broadcasted_iota(jnp.int32, (64, 128), 1) < 64

    def rows_of(v, l, p):
        return wide[v, l, pl.ds(p * 64, 64), :]

    def pair(slot, n):
        found = []
        tiles = []
        for w in range(2):
            l = tab_ref[0, w * chips + slot]
            p = tab_ref[1, w * chips + slot]
            mat = blk[w * chips + slot]
            ys = [rows_of(v, l, p) for v in range(vectors)]
            tiles.append(ys)
            lhs = jnp.concatenate(
                [jnp.where(low64, y, 0.0).astype(BF16) for y in ys]
                + [jnp.where(low64, 0.0, y).astype(BF16) for y in ys], axis=0
            )
            inner = lax.dot_general(
                lhs, mat, (((1,), (1,)), ((), ())), preferred_element_type=F32
            ).astype(BF16)
            rhs = jnp.concatenate(
                [
                    jnp.concatenate(
                        [inner[v * 64:(v + 1) * 64], inner[(vectors + v) * 64:(vectors + v + 1) * 64]],
                        axis=0,
                    )
                    for v in range(vectors)
                ],
                axis=1,
            )
            out = jnp.dot(lefts[l], rhs, preferred_element_type=F32)
            sums = []
            for v in range(vectors):
                top = out[0:64, v * 128:(v + 1) * 128]
                bottom = out[64:128, v * 128:(v + 1) * 128]
                if w == 0:
                    sums.append(top + pltpu.roll(bottom, 64, 1))
                else:
                    sums.append(pltpu.roll(top, 64, 1) + bottom)
            found.append(sums)
        parts = []
        for v in range(vectors):
            part = jnp.where(low64, found[0][v], found[1][v]).astype(BF16).astype(F32)
            stage[lax.rem(n, 4), v] = part
            parts.append(part)
        for v in range(vectors):
            both = jnp.where(low64, tiles[0][v], tiles[1][v])
            for w in range(vectors):
                prod = (both * parts[w]).reshape(8, 8, 128)
                acc[v * vectors + w] += jnp.sum(prod, axis=0)

    low4 = lax.broadcasted_iota(jnp.int32, (8, 8, 128), 1) < 4

    def op_copy(step, batch):
        peer = op_peer(step)
        return pltpu.make_async_remote_copy(
            src_ref=outbox.at[batch, peer],
            dst_ref=inbox.at[batch, op],
            send_sem=op_send.at[batch],
            recv_sem=op_recv.at[batch],
            device_id={"op": peer},
            device_id_type=MESH,
        )

    def finish(batch):
        for v in range(vectors):
            xs = [stage[j, v].reshape(8, 8, 128) for j in range(4)]
            ev, od = [], []
            for j in (0, 2):
                x, y = xs[j], xs[j + 1]
                ev.append(jnp.where(low4, x, pltpu.roll(y, 4, 1)))
                od.append(jnp.where(low4, pltpu.roll(x, 4, 1), y))
            even = jnp.concatenate(ev, axis=1).astype(BF16)
            odd = jnp.concatenate(od, axis=1).astype(BF16)
            for t in range(8):
                outbox[batch, 2 * t, v * 16:(v + 1) * 16, :] = even[t]
                outbox[batch, 2 * t + 1, v * 16:(v + 1) * 16, :] = odd[t]
        if groups > 1:

            def send(step, carry):
                op_copy(step, batch).start()
                return carry

            lax.fori_loop(1, groups, send, 0)
        inbox[batch, op] = outbox[batch, op]

    def gather_sum(batch):
        if groups > 1:
            pltpu.make_async_remote_copy(
                src_ref=outbox.at[batch, pl.ds(0, groups - 1)],
                dst_ref=inbox.at[batch, pl.ds(0, groups - 1)],
                send_sem=op_send.at[batch],
                recv_sem=op_recv.at[batch],
                device_id={"op": op_peer(1)},
                device_id_type=MESH,
            ).wait()
        value = inbox[batch, 0].astype(F32)
        for g in range(1, groups):
            value += inbox[batch, g].astype(F32)
        total[batch] = value.astype(BF16)

    def turn(h, carry):
        def serve(q):
            for way in range(2):
                ring_copy(way, h, q).wait_recv()
                if last_way(q) == way:
                    ring_copy(way, h + 1, q).start()
                else:

                    @pl.when(h < half - 1)
                    def _():
                        ring_copy(way, h + 1, q).start()

        for q in range(CHUNKS // 2):
            serve(q)
        pair_copy(h - 1).wait_recv()
        first = 2 * (h - 1) - 1 + lax.div(half - h, half - 1)
        pair(h - 1, first)

        @pl.when(jnp.logical_and(lax.rem(h, 2) == 1, h >= 3))
        def _():
            finish(lax.div(h - 3, 2))

        for q in range(CHUNKS // 2, CHUNKS):
            serve(q)

        @pl.when(h >= 2)
        def _():
            pair_copy(chips - (h - 1)).wait_recv()
            pair(chips - (h - 1), 2 * (h - 1))

        choose(h)
        choose(chips - h)

        @pl.when(jnp.logical_and(lax.rem(h, 2) == 1, h >= 5))
        def _():
            gather_sum(lax.div(h - 5, 2))

        return carry

    lax.fori_loop(1, half, turn, 0)

    for q in range(CHUNKS):
        ring_copy(last_way(q), half, q).wait_recv()
    choose(half)
    pair_copy(half - 1).wait_recv()
    pair(half - 1, 2 * half - 3)
    pair_copy(half + 1).wait_recv()
    pair(half + 1, 2 * half - 2)
    pair_copy(half).wait_recv()
    pair(half, 2 * half - 1)
    finish(batches - 1)

    dots[...] = jnp.zeros_like(dots)
    for i in range(vectors * vectors):
        dots[i:i + 1, :] = jnp.sum(acc[i], axis=0, keepdims=True)
    if groups > 1:

        def dot_copy(step):
            return pltpu.make_async_remote_copy(
                src_ref=dots,
                dst_ref=dots_op.at[op],
                send_sem=dot_send.at[0],
                recv_sem=dot_recv.at[0],
                device_id={"op": op_peer(step)},
                device_id_type=MESH,
            )

        def send_dots(step, carry):
            dot_copy(step).start()
            return carry

        lax.fori_loop(1, groups, send_dots, 0)
    dots_op[op] = dots[...]

    if batches > 1:
        gather_sum(batches - 2)

    if groups > 1:
        pltpu.make_async_remote_copy(
            src_ref=dots_op.at[pl.ds(0, groups - 1)],
            dst_ref=dots_op.at[pl.ds(0, groups - 1)],
            send_sem=dot_send.at[0],
            recv_sem=dot_recv.at[0],
            device_id={"op": op_peer(1)},
            device_id_type=MESH,
        ).wait()
    value = dots_op[0]
    for g in range(1, groups):
        value += dots_op[g]
    one[...] = value
    core_copy = pltpu.make_async_remote_copy(
        src_ref=one,
        dst_ref=dots_core,
        send_sem=dot_send.at[1],
        recv_sem=dot_recv.at[1],
        device_id={"sec": mate},
        device_id_type=MESH,
    )
    core_copy.start()
    gather_sum(batches - 1)
    core_copy.wait()
    two[...] = one[...] + dots_core[...]

    def send_chip(step, carry):
        pltpu.make_async_remote_copy(
            src_ref=two,
            dst_ref=dots_chip.at[z],
            send_sem=dot_send.at[2],
            recv_sem=dot_recv.at[2],
            device_id={"sec": chip(step)},
            device_id_type=MESH,
        ).start()
        return carry

    lax.fori_loop(1, chips, send_chip, 0)
    dots_chip[z] = two[...]

    code = idx_ref[...]
    second = lax.rem(code, 2) == 1
    base = lax.div(code, 2) * 4
    column = lax.broadcasted_iota(jnp.int32, (64, 128), 1)
    rows = total.shape[0] * 16
    for v in range(vectors):
        table = total[:, v * 16:(v + 1) * 16, :].reshape(rows, 128)
        got = []
        for i in range(4):
            hot = jnp.where(column[:idx_ref.shape[0], :rows] == base[:, :rows] + i, 1.0, 0.0).astype(BF16)
            got.append(jnp.dot(hot, table, preferred_element_type=F32))
        lanes = column[:idx_ref.shape[0]] < 64
        for i in range(2):
            x = jnp.where(second, pltpu.roll(got[2 * i], 64, 1), got[2 * i])
            y = jnp.where(second, got[2 * i + 1], pltpu.roll(got[2 * i + 1], 64, 1))
            sig_ref[v, :, i * 128:(i + 1) * 128] = jnp.where(lanes, x, y).astype(BF16)

    def drain(h, carry):
        for q in range(CHUNKS):
            for way in range(2):
                if last_way(q) == way:
                    ring_copy(way, h, q).wait_send()
                else:

                    @pl.when(h < half)
                    def _():
                        ring_copy(way, h, q).wait_send()

        return carry

    lax.fori_loop(1, half + 1, drain, 0)

    def drain_pairs(slot, carry):
        pair_copy(slot).wait_send()
        return carry

    lax.fori_loop(0, chips, drain_pairs, 0)

    pltpu.make_async_remote_copy(
        src_ref=dots_chip.at[pl.ds(0, chips - 1)],
        dst_ref=dots_chip.at[pl.ds(0, chips - 1)],
        send_sem=dot_send.at[2],
        recv_sem=dot_recv.at[2],
        device_id={"sec": chip(1)},
        device_id_type=MESH,
    ).wait()
    value = dots_chip[0]
    for g in range(1, chips):
        value += dots_chip[g]
    three[...] = jnp.sum(value, axis=1, keepdims=True) * scale
    for v in range(vectors):
        for w in range(vectors):
            i = v * vectors + w
            sub_ref[v:v + 1, w:w + 1] = three[i:i + 1, :]


def body(psi, left_ops, right_ops, dest_dev, right_sub):
    vectors, secs, pairs, cells = psi.shape
    terms = left_ops.shape[0]
    devices = lax.axis_size("sec")
    groups = lax.axis_size("op")
    chips = devices // 2
    count = secs * pairs
    me = lax.axis_index("sec")
    core = me % 2
    z = me // 2
    all_dest = dest_dev.reshape(devices, count)
    all_sub = right_sub.reshape(devices, count)
    my_dest = lax.dynamic_index_in_dim(all_dest, me, 0, keepdims=False)
    my_sub = lax.dynamic_index_in_dim(all_sub, me, 0, keepdims=False)
    mate = z * 2 + 1 - core
    mate_dest = lax.dynamic_index_in_dim(all_dest, mate, 0, keepdims=False)
    mate_sub = lax.dynamic_index_in_dim(all_sub, mate, 0, keepdims=False)
    slots = jnp.arange(chips, dtype=jnp.int32)
    source = ((z - slots + chips) % chips) * 2
    same = source + core
    both = jnp.concatenate([same, source + 1 - core])
    places = jnp.arange(count, dtype=jnp.int32)
    hit = both[:, None] == my_dest[None, :]
    where = jnp.sum(jnp.where(hit, places[None, :], 0), axis=1)
    mine = jnp.sum(jnp.where(hit[:chips], my_sub[None, :], 0), axis=1)
    theirs = jnp.sum(
        jnp.where(same[:, None] == mate_dest[None, :], mate_sub[None, :], 0), axis=1
    )
    tab = jnp.stack([where // pairs, where % pairs, jnp.concatenate([mine, theirs])])
    slot = (z - my_dest // 2 + chips) % chips
    half = chips // 2
    order = jnp.where(
        slot == 0, 0, jnp.where(slot == half, chips - 1, jnp.where(slot < half, 2 * slot - 1, 2 * (chips - slot)))
    )
    code = order * 2 + (my_dest % 2 != core).astype(jnp.int32)
    idx = jnp.broadcast_to(code[:, None], (count, 128))
    entries = secs * devices * pairs * cells
    batches = chips // 4
    vmem = pltpu.VMEM
    dma = pltpu.SemaphoreType.DMA
    sigma, subspace = pl.pallas_call(
        functools.partial(kernel, chips, groups, 1.0 / entries),
        out_shape=(
            jax.ShapeDtypeStruct((vectors, count, cells // 16), BF16),
            jax.ShapeDtypeStruct((vectors, vectors), F32),
        ),
        in_specs=[pl.BlockSpec(memory_space=pltpu.SMEM)]
        + [pl.BlockSpec(memory_space=pltpu.VMEM)] * 4,
        out_specs=(pl.BlockSpec(memory_space=pltpu.VMEM), pl.BlockSpec(memory_space=pltpu.VMEM)),
        scratch_shapes=[
            vmem((chips, secs, 128, 128), BF16),
            vmem((2 * chips, 128, 128), BF16),
            vmem((chips, 128, 128), BF16),
            vmem((vectors, secs, pairs * 64, 128), F32),
            vmem((secs, 128, 128), BF16),
            vmem((4, vectors, 64, 128), F32),
            vmem((batches, 16, vectors * 16, 128), BF16),
            vmem((batches, groups, vectors * 16, 128), BF16),
            vmem((batches, vectors * 16, 128), BF16),
            vmem((vectors * vectors, 8, 128), F32),
            vmem((16, 128), F32),
            vmem((groups, 16, 128), F32),
            vmem((16, 128), F32),
            vmem((chips, 16, 128), F32),
            vmem((16, 128), F32),
            vmem((16, 128), F32),
            vmem((16, 1), F32),
            vmem((secs, 128, 128), BF16),
            dma((2, half + 1, CHUNKS)),
            dma((2, half + 1, CHUNKS)),
            dma((chips,)),
            dma((chips,)),
            dma((batches,)),
            dma((batches,)),
            dma((3,)),
            dma((3,)),
        ],
        compiler_params=pltpu.CompilerParams(
            collective_id=0, has_side_effects=True, vmem_limit_bytes=48 * 1024 * 1024
        ),
        cost_estimate=pl.CostEstimate(
            flops=4 * terms * vectors * count * 64 ** 3, bytes_accessed=8 << 20, transcendentals=0
        ),
    )(tab, idx, psi, left_ops, right_ops)
    return sigma.reshape(vectors, secs, pairs, cells // 16), subspace


def solution(mesh):
    return jax.shard_map(
        body,
        mesh=mesh,
        in_specs=(
            P(None, "sec", None, None),
            P("op", "sec", None, None),
            P("op", "sec", None, None),
            P(),
            P(),
        ),
        out_specs=(P(None, "sec", None, "op"), P()),
        check_vma=False,
    )
```

```python
import functools

import jax
import jax.numpy as jnp
from jax import lax
from jax.experimental import pallas as pl
from jax.experimental.pallas import tpu as pltpu
from jax.sharding import PartitionSpec as P

MESH = pl.DeviceIdType.MESH
CHUNKS = 2
FAR = 4
F32 = jnp.float32
BF16 = jnp.bfloat16


def kernel(
    chips, groups, scale,
    psi_hbm, left_hbm, right_hbm, dest_hbm, choice_hbm,
    sig_ref, sub_ref,
    psi_ref, left_ref, right_ref, dest_ref, choice_ref, lists, tab_ref, code_ref, ring, far, blk, pass_on, wide, lefts, stage, outbox, inbox, total, acc,
    dots, dots_op, dots_core, dots_chip, one, two, shelf,
    load_sem, ring_send, ring_recv, far_send, far_recv, pair_send, pair_recv, op_send, op_recv, dot_send, dot_recv,
):
    half = chips // 2
    near = half - FAR
    vectors, secs, pairs, cells = psi_ref.shape
    batches = chips // 4
    per = secs // CHUNKS
    me = lax.axis_index("sec")
    core = lax.rem(me, 2)
    z = lax.div(me, 2)
    op = lax.axis_index("op")
    mate = z * 2 + 1 - core

    def chip(step):
        return lax.rem(z + step + chips, chips) * 2 + core

    def op_peer(step):
        return lax.rem(op + step, groups)

    loads = [
        pltpu.make_async_copy(src, dst, load_sem.at[i])
        for i, (src, dst) in enumerate(
            (
                (right_hbm, right_ref),
                (dest_hbm, dest_ref),
                (choice_hbm, choice_ref),
                (psi_hbm, psi_ref),
                (left_hbm, left_ref),
            )
        )
    ]
    for load in loads:
        load.start()

    barrier = pltpu.get_barrier_semaphore()

    def greet(where):
        pl.semaphore_signal(barrier, inc=1, device_id=where, device_id_type=MESH)

    def greet_op(step, carry):
        greet({"op": op_peer(step)})
        return carry

    greet({"sec": chip(1)})
    greet({"sec": chip(-1)})
    greet({"sec": mate})
    if groups > 1:
        lax.fori_loop(1, groups, greet_op, 0)
    greetings = 3 + (groups - 1)

    def pack_right(s, carry):
        for high in range(2):
            ring[0, s, high * 64:(high + 1) * 64, :] = jnp.concatenate(
                [right_ref[2 * high, s], right_ref[2 * high + 1, s]], axis=1
            )
        return carry

    loads[0].wait()
    lax.fori_loop(0, secs, pack_right, 0)
    rows = 4 * chips
    loads[1].wait()
    loads[2].wait()
    total_secs = dest_ref.shape[1]
    width = min(128, total_secs)
    if width == 128:
        start = pl.multiple_of(lax.div(me * secs, width) * width, width)
    else:
        start = 0
    near_dest = dest_ref[:, pl.ds(start, width)]
    near_choice = choice_ref[:, pl.ds(start, width)]

    def step_of(shape):
        return lax.shift_right_logical(lax.broadcasted_iota(jnp.int32, shape, 0), 2)

    def source_of(n):
        odd = lax.rem(n, 2)
        half_n = lax.shift_right_logical(n + odd, 1)
        slot = jnp.where(odd == 1, half_n, chips - half_n)
        return lax.rem(z - slot + 2 * chips, chips) * 2

    source = source_of(step_of((rows, width)))
    sector = lax.broadcasted_iota(jnp.int32, (1, width), 1) + start
    holder = lax.div(sector, secs)
    inside = lax.rem(sector, secs)
    count = secs * pairs
    block_l = lax.div(lax.broadcasted_iota(jnp.int32, (count, width), 0), pairs)
    block_p = lax.rem(lax.broadcasted_iota(jnp.int32, (count, width), 0), pairs)
    found = [jnp.zeros((rows, width), jnp.int32) for _ in range(4)]
    target = jnp.zeros((count, width), jnp.int32)
    for p in range(pairs):
        here = jnp.where(holder == me, near_dest[p:p + 1], -1)
        there = jnp.where(holder == mate, near_dest[p:p + 1], -1)
        pick = near_choice[p:p + 1]
        hits = (here == source + core, here == source + 1 - core, there == source + core)
        place = inside * pairs + p
        found[0] += jnp.where(hits[0], place, 0)
        found[1] += jnp.where(hits[1], place, 0)
        found[2] += jnp.where(hits[0], pick, 0)
        found[3] += jnp.where(hits[2], pick, 0)
        fits = jnp.where(block_l == inside, jnp.where(block_p == p, 1, 0), 0)
        target += fits * jnp.where(holder == me, near_dest[p:p + 1], 0)
    lane_of = lax.broadcasted_iota(jnp.int32, (rows, 128), 1)
    table = jnp.zeros((rows, 128), jnp.int32)
    for k in range(4):
        most = count - 1 if k < 2 else secs - 1
        value = jnp.minimum(jnp.sum(found[k], axis=1, keepdims=True), most)
        table += jnp.where(lane_of == k, value, 0)
    lists[0:rows, :] = table
    owner = lax.div(lax.broadcasted_iota(jnp.int32, (pairs, total_secs), 1), secs)
    for way in range(2):
        sign = 1 - 2 * way
        origin = lax.rem(z - sign * near + 2 * chips, chips) * 2 + core
        from_there = jnp.where(dest_ref[...] == origin, choice_ref[...], 0)
        for j in range(2 * FAR - 1):
            taker = lax.rem(z + sign * (j // 2 + 1) + chips, chips) * 2
            taker += core if j % 2 == (0 if j < 2 * FAR - 2 else way) else 1 - core
            wanted = jnp.where(owner == taker, from_there, 0)
            wanted = jnp.sum(jnp.sum(wanted, axis=0, keepdims=True), axis=1, keepdims=True)
            wanted = jnp.minimum(wanted, secs - 1)
            at = rows + way * (2 * FAR - 1) + j
            lists[at:at + 1, :] = jnp.broadcast_to(wanted, (1, 128))
    to_scalars = pltpu.make_async_copy(lists, tab_ref, load_sem.at[5])
    to_scalars.start()
    goal = jnp.sum(target, axis=1, keepdims=True)
    slot = lax.rem(z - lax.shift_right_logical(goal, 1) + chips, chips)
    order = jnp.where(slot < half, 2 * slot - 1, 2 * (chips - slot))
    order = jnp.where(slot == 0, 0, jnp.where(slot == half, chips - 1, order))
    code = order * 2 + jnp.where(lax.rem(goal, 2) == core, 0, 1)
    code_ref[...] = jnp.broadcast_to(code, (count, 128))
    pl.semaphore_wait(barrier, greetings)

    def ring_copy(way, hop, q):
        if way == 0:
            src, dst, target = hop - 1, hop, chip(1)
        else:
            src, dst, target = lax.rem(chips + 1 - hop, chips), chips - hop, chip(-1)
        return pltpu.make_async_remote_copy(
            src_ref=ring.at[src, pl.ds(q * per, per)],
            dst_ref=ring.at[dst, pl.ds(q * per, per)],
            send_sem=ring_send.at[way, hop, q],
            recv_sem=ring_recv.at[way, hop, q],
            device_id={"sec": target},
            device_id_type=MESH,
        )

    def far_copy(way, j):
        step = j // 2 + 1
        other = j % 2 if j < 2 * FAR - 2 else way
        slot = near + step if way == 0 else chips - near - step
        taker = lax.rem(z + (1 - 2 * way) * step + chips, chips) * 2
        return pltpu.make_async_remote_copy(
            src_ref=far.at[way, j],
            dst_ref=blk.at[other * chips + slot],
            send_sem=far_send.at[way, j],
            recv_sem=pair_recv.at[slot] if other else far_recv.at[slot],
            device_id={"sec": taker + (1 - core if other else core)},
            device_id_type=MESH,
        )

    def far_arrived(slot):
        pltpu.make_async_remote_copy(
            src_ref=far.at[0, 0],
            dst_ref=blk.at[slot],
            send_sem=far_send.at[0, 0],
            recv_sem=far_recv.at[slot],
            device_id={"sec": mate},
            device_id_type=MESH,
        ).wait_recv()

    for q in range(CHUNKS):
        ring_copy(0, 1, q).start()
        ring_copy(1, 1, q).start()

    def pair_copy(slot):
        return pltpu.make_async_remote_copy(
            src_ref=pass_on.at[slot],
            dst_ref=blk.at[chips + slot],
            send_sem=pair_send.at[slot],
            recv_sem=pair_recv.at[slot],
            device_id={"sec": mate},
            device_id_type=MESH,
        )

    def shelve(slot):
        for s in range(secs):
            shelf[s] = ring[slot, s]

    def choose(slot, n):
        pass_on[slot] = shelf[tab_ref[4 * n, 3]]
        pair_copy(slot).start()
        blk[slot] = shelf[tab_ref[4 * n, 2]]

    def choose_far(way):
        takers = 2 * FAR - 1
        for j in reversed(range(takers)):
            far[way, j] = shelf[tab_ref[rows + way * takers + j, 0]]
            far_copy(way, j).start()

    to_scalars.wait()

    shelve(0)
    choose(0, 0)

    low = lax.broadcasted_iota(jnp.int32, (pairs, 128), 1) < 64

    def widen(step, carry):
        v = lax.div(step, secs)
        l = lax.rem(step, secs)
        for t in range(cells // 128):
            x = psi_ref[v, l, :, t * 128:(t + 1) * 128].astype(F32)
            r = pltpu.roll(x, 64, 1)
            wide[v, pl.ds(l * (pairs * 64) + 2 * t, pairs, stride=64), :] = jnp.where(low, x, r)
            wide[v, pl.ds(l * (pairs * 64) + 2 * t + 1, pairs, stride=64), :] = jnp.where(low, r, x)
        return carry

    loads[3].wait()
    lax.fori_loop(0, vectors * secs, widen, 0)

    def pack_left(l, carry):
        for high in range(2):
            lefts[l, high * 64:(high + 1) * 64, :] = jnp.concatenate(
                [left_ref[2 * high, l], left_ref[2 * high + 1, l]], axis=1
            )
        return carry

    loads[4].wait()
    lax.fori_loop(0, secs, pack_left, 0)
    acc[...] = jnp.zeros_like(acc)
    low64 = lax.broadcasted_iota(jnp.int32, (64, 128), 1) < 64

    def rows_of(v, place):
        return wide[v, pl.ds(place * 64, 64), :]

    def pair(slot, n):
        found = []
        tiles = []
        for w in range(2):
            place = tab_ref[4 * n, w]
            l = lax.div(place, pairs)
            mat = blk[w * chips + slot]
            ys = [rows_of(v, place) for v in range(vectors)]
            tiles.append(ys)
            lhs = jnp.concatenate(
                [jnp.where(low64, y, 0.0).astype(BF16) for y in ys]
                + [jnp.where(low64, 0.0, y).astype(BF16) for y in ys], axis=0
            )
            inner = lax.dot_general(
                lhs, mat, (((1,), (1,)), ((), ())), preferred_element_type=F32
            ).astype(BF16)
            rhs = jnp.concatenate(
                [
                    jnp.concatenate(
                        [inner[v * 64:(v + 1) * 64], inner[(vectors + v) * 64:(vectors + v + 1) * 64]],
                        axis=0,
                    )
                    for v in range(vectors)
                ],
                axis=1,
            )
            out = jnp.dot(lefts[l], rhs, preferred_element_type=F32)
            sums = []
            for v in range(vectors):
                top = out[0:64, v * 128:(v + 1) * 128]
                bottom = out[64:128, v * 128:(v + 1) * 128]
                if w == 0:
                    sums.append(top + pltpu.roll(bottom, 64, 1))
                else:
                    sums.append(pltpu.roll(top, 64, 1) + bottom)
            found.append(sums)
        parts = []
        for v in range(vectors):
            part = jnp.where(low64, found[0][v], found[1][v]).astype(BF16).astype(F32)
            stage[lax.rem(n, 4), v] = part
            parts.append(part)
        for v in range(vectors):
            both = jnp.where(low64, tiles[0][v], tiles[1][v])
            for w in range(vectors):
                prod = (both * parts[w]).reshape(8, 8, 128)
                acc[v * vectors + w] += jnp.sum(prod, axis=0)

    low4 = lax.broadcasted_iota(jnp.int32, (8, 8, 128), 1) < 4

    def op_copy(step, batch):
        peer = op_peer(step)
        return pltpu.make_async_remote_copy(
            src_ref=outbox.at[batch, peer],
            dst_ref=inbox.at[batch, op],
            send_sem=op_send.at[batch],
            recv_sem=op_recv.at[batch],
            device_id={"op": peer},
            device_id_type=MESH,
        )

    def finish(batch):
        for v in range(vectors):
            xs = [stage[j, v].reshape(8, 8, 128) for j in range(4)]
            ev, od = [], []
            for j in (0, 2):
                x, y = xs[j], xs[j + 1]
                ev.append(jnp.where(low4, x, pltpu.roll(y, 4, 1)))
                od.append(jnp.where(low4, pltpu.roll(x, 4, 1), y))
            even = jnp.concatenate(ev, axis=1).astype(BF16)
            odd = jnp.concatenate(od, axis=1).astype(BF16)
            for t in range(8):
                outbox[batch, 2 * t, v * 16:(v + 1) * 16, :] = even[t]
                outbox[batch, 2 * t + 1, v * 16:(v + 1) * 16, :] = odd[t]
        if groups > 1:

            def send(step, carry):
                op_copy(step, batch).start()
                return carry

            lax.fori_loop(1, groups, send, 0)
        inbox[batch, op] = outbox[batch, op]

    def gather_sum(batch):
        if groups > 1:
            pltpu.make_async_remote_copy(
                src_ref=outbox.at[batch, pl.ds(0, groups - 1)],
                dst_ref=inbox.at[batch, pl.ds(0, groups - 1)],
                send_sem=op_send.at[batch],
                recv_sem=op_recv.at[batch],
                device_id={"op": op_peer(1)},
                device_id_type=MESH,
            ).wait()
        value = inbox[batch, 0].astype(F32)
        for g in range(1, groups):
            value += inbox[batch, g].astype(F32)
        total[batch] = value.astype(BF16)

    def first_pair(h):
        pair_copy(h - 1).wait_recv()

        @pl.when(h - 1 > near)
        def _():
            far_arrived(h - 1)

        pair(h - 1, 2 * (h - 1) - 1 + lax.div(half - h, half - 1))

        @pl.when(jnp.logical_and(lax.rem(h, 2) == 1, h >= 3))
        def _():
            finish(lax.div(h - 3, 2))

    def second_pair(h):
        @pl.when(h >= 2)
        def _():
            pair_copy(chips - (h - 1)).wait_recv()

            @pl.when(h - 1 > near)
            def _():
                far_arrived(chips - (h - 1))

            pair(chips - (h - 1), 2 * (h - 1))

        @pl.when(jnp.logical_and(lax.rem(h, 2) == 1, h >= 5))
        def _():
            gather_sum(lax.div(h - 5, 2))

    def turn(h, carry):
        def serve(q):
            for way in range(2):
                ring_copy(way, h, q).wait_recv()

                @pl.when(h < near)
                def _():
                    ring_copy(way, h + 1, q).start()

        for q in range(CHUNKS // 2):
            serve(q)
        first_pair(h)
        for q in range(CHUNKS // 2, CHUNKS):
            serve(q)
        for way in range(2):
            slot = h if way == 0 else chips - h
            shelve(slot)

            @pl.when(h == near)
            def _():
                choose_far(way)

            choose(slot, 2 * h - 1 + way)
        second_pair(h)
        return carry

    lax.fori_loop(1, near + 1, turn, 0)

    def far_turn(h, carry):
        first_pair(h)
        second_pair(h)
        return carry

    lax.fori_loop(near + 1, half, far_turn, 0)

    for slot, n in ((half - 1, 2 * half - 3), (half + 1, 2 * half - 2), (half, 2 * half - 1)):
        pair_copy(slot).wait_recv()
        far_arrived(slot)
        pair(slot, n)

    lane = lax.broadcasted_iota(jnp.int32, (1, 128), 1)
    row = jnp.zeros((1, 128), F32)
    for i in range(vectors * vectors):
        whole = jnp.sum(jnp.sum(acc[i], axis=0, keepdims=True), axis=1, keepdims=True)
        row += jnp.where(lane == i, whole, 0.0)
    dots[...] = row
    if groups > 1:

        def dot_copy(step):
            return pltpu.make_async_remote_copy(
                src_ref=dots,
                dst_ref=dots_op.at[op],
                send_sem=dot_send.at[0],
                recv_sem=dot_recv.at[0],
                device_id={"op": op_peer(step)},
                device_id_type=MESH,
            )

        def send_dots(step, carry):
            dot_copy(step).start()
            return carry

        lax.fori_loop(1, groups, send_dots, 0)
    dots_op[op] = dots[...]
    finish(batches - 1)

    if groups > 1:
        pltpu.make_async_remote_copy(
            src_ref=dots_op.at[pl.ds(0, groups - 1)],
            dst_ref=dots_op.at[pl.ds(0, groups - 1)],
            send_sem=dot_send.at[0],
            recv_sem=dot_recv.at[0],
            device_id={"op": op_peer(1)},
            device_id_type=MESH,
        ).wait()
    value = dots_op[0]
    for g in range(1, groups):
        value += dots_op[g]
    one[...] = value
    core_copy = pltpu.make_async_remote_copy(
        src_ref=one,
        dst_ref=dots_core,
        send_sem=dot_send.at[1],
        recv_sem=dot_recv.at[1],
        device_id={"sec": mate},
        device_id_type=MESH,
    )
    core_copy.start()
    if batches > 1:
        gather_sum(batches - 2)
    core_copy.wait()
    two[...] = one[...] + dots_core[...]

    def send_chip(step, carry):
        pltpu.make_async_remote_copy(
            src_ref=two,
            dst_ref=dots_chip.at[z],
            send_sem=dot_send.at[2],
            recv_sem=dot_recv.at[2],
            device_id={"sec": chip(step)},
            device_id_type=MESH,
        ).start()
        return carry

    def send_chips(step, carry):
        send_chip(half - step, 0)
        send_chip(half + step, 0)
        return carry

    send_chip(half, 0)
    lax.fori_loop(1, half, send_chips, 0)
    dots_chip[z] = two[...]
    gather_sum(batches - 1)

    code = code_ref[...]
    second = lax.rem(code, 2) == 1
    base = lax.div(code, 2) * 4
    column = lax.broadcasted_iota(jnp.int32, (64, 128), 1)
    for v in range(vectors):
        table = total[:, v * 16:(v + 1) * 16, :].reshape(rows, 128)
        got = []
        for i in range(4):
            hot = jnp.where(column[:count, :rows] == base[:, :rows] + i, 1.0, 0.0).astype(BF16)
            got.append(jnp.dot(hot, table, preferred_element_type=F32))
        lanes = column[:count] < 64
        for i in range(2):
            x = jnp.where(second, pltpu.roll(got[2 * i], 64, 1), got[2 * i])
            y = jnp.where(second, got[2 * i + 1], pltpu.roll(got[2 * i + 1], 64, 1))
            sig_ref[v, :, i * 128:(i + 1) * 128] = jnp.where(lanes, x, y).astype(BF16)

    def drain(h, carry):
        for q in range(CHUNKS):
            for way in range(2):
                ring_copy(way, h, q).wait_send()
        return carry

    lax.fori_loop(1, near + 1, drain, 0)

    for way in range(2):
        for j in range(2 * FAR - 1):
            far_copy(way, j).wait_send()

    def drain_pairs(slot, carry):
        pair_copy(slot).wait_send()
        return carry

    lax.fori_loop(0, near + 1, drain_pairs, 0)
    lax.fori_loop(chips - near, chips, drain_pairs, 0)

    pltpu.make_async_remote_copy(
        src_ref=dots_chip.at[pl.ds(0, chips - 1)],
        dst_ref=dots_chip.at[pl.ds(0, chips - 1)],
        send_sem=dot_send.at[2],
        recv_sem=dot_recv.at[2],
        device_id={"sec": chip(1)},
        device_id_type=MESH,
    ).wait()
    value = dots_chip[0]
    for g in range(1, chips):
        value += dots_chip[g]
    value = value * scale
    for v in range(vectors):
        for w in range(vectors):
            i = v * vectors + w
            sub_ref[v:v + 1, w:w + 1] = value[:, i:i + 1]


def body(psi, left_ops, right_ops, dest_dev, right_sub):
    vectors, secs, pairs, cells = psi.shape
    terms = left_ops.shape[0]
    devices = lax.axis_size("sec")
    groups = lax.axis_size("op")
    chips = devices // 2
    count = secs * pairs
    half = chips // 2
    entries = secs * devices * pairs * cells
    batches = chips // 4
    vmem = pltpu.VMEM
    dma = pltpu.SemaphoreType.DMA
    sigma, subspace = pl.pallas_call(
        functools.partial(kernel, chips, groups, 1.0 / entries),
        out_shape=(
            jax.ShapeDtypeStruct((vectors, count, cells // 16), BF16),
            jax.ShapeDtypeStruct((vectors, vectors), F32),
        ),
        in_specs=[pl.BlockSpec(memory_space=pl.ANY)] * 5,
        out_specs=(pl.BlockSpec(memory_space=pltpu.VMEM), pl.BlockSpec(memory_space=pltpu.VMEM)),
        scratch_shapes=[
            vmem(psi.shape, BF16),
            vmem(left_ops.shape, BF16),
            vmem(right_ops.shape, BF16),
            vmem((pairs, secs * devices), jnp.int32),
            vmem((pairs, secs * devices), jnp.int32),
            vmem((4 * chips + 16, 128), jnp.int32),
            pltpu.SMEM((4 * chips + 16, 128), jnp.int32),
            vmem((count, 128), jnp.int32),
            vmem((chips, secs, 128, 128), BF16),
            vmem((2, 2 * FAR - 1, 128, 128), BF16),
            vmem((2 * chips, 128, 128), BF16),
            vmem((chips, 128, 128), BF16),
            vmem((vectors, count * 64, 128), F32),
            vmem((secs, 128, 128), BF16),
            vmem((4, vectors, 64, 128), F32),
            vmem((batches, 16, vectors * 16, 128), BF16),
            vmem((batches, groups, vectors * 16, 128), BF16),
            vmem((batches, vectors * 16, 128), BF16),
            vmem((vectors * vectors, 8, 128), F32),
            vmem((1, 128), F32),
            vmem((groups, 1, 128), F32),
            vmem((1, 128), F32),
            vmem((chips, 1, 128), F32),
            vmem((1, 128), F32),
            vmem((1, 128), F32),
            vmem((secs, 128, 128), BF16),
            dma((6,)),
            dma((2, half + 1, CHUNKS)),
            dma((2, half + 1, CHUNKS)),
            dma((2, 2 * FAR - 1)),
            dma((chips,)),
            dma((chips,)),
            dma((chips,)),
            dma((batches,)),
            dma((batches,)),
            dma((3,)),
            dma((3,)),
        ],
        compiler_params=pltpu.CompilerParams(
            collective_id=0, has_side_effects=True, vmem_limit_bytes=56 * 1024 * 1024
        ),
        cost_estimate=pl.CostEstimate(
            flops=4 * terms * vectors * count * 64 ** 3, bytes_accessed=8 << 20, transcendentals=0
        ),
    )(psi, left_ops, right_ops, dest_dev.T, right_sub.T)
    return sigma.reshape(vectors, secs, pairs, cells // 16), subspace


def solution(mesh):
    return jax.shard_map(
        body,
        mesh=mesh,
        in_specs=(
            P(None, "sec", None, None),
            P("op", "sec", None, None),
            P("op", "sec", None, None),
            P(),
            P(),
        ),
        out_specs=(P(None, "sec", None, "op"), P()),
        check_vma=False,
    )
```

```python
import functools

import jax
import jax.numpy as jnp
from jax import lax
from jax.experimental import pallas as pl
from jax.experimental.pallas import tpu as pltpu
from jax.sharding import PartitionSpec as P

MESH = pl.DeviceIdType.MESH
CHUNKS = 2
FAR = 4
F32 = jnp.float32
BF16 = jnp.bfloat16


def kernel(
    chips, groups, scale,
    psi_hbm, left_hbm, right_hbm, dest_hbm, choice_hbm,
    sig_ref, sub_ref,
    psi_ref, left_ref, right_ref, dest_ref, choice_ref, lists, tab_ref, code_ref, ring, far, blk, pass_on, wide, lefts, stage, outbox, inbox, total, acc,
    dots, dots_op, dots_core, dots_chip, one, two, shelf,
    load_sem, ring_send, ring_recv, far_send, far_recv, pair_send, pair_recv, op_send, op_recv, dot_send, dot_recv,
):
    half = chips // 2
    near = half - FAR
    vectors, secs, pairs, cells = psi_ref.shape
    batches = chips // 4
    per = secs // CHUNKS
    me = lax.axis_index("sec")
    core = lax.rem(me, 2)
    z = lax.div(me, 2)
    op = lax.axis_index("op")
    mate = z * 2 + 1 - core

    def chip(step):
        return lax.rem(z + step + chips, chips) * 2 + core

    def op_peer(step):
        return lax.rem(op + step, groups)

    loads = [
        pltpu.make_async_copy(src, dst, load_sem.at[i])
        for i, (src, dst) in enumerate(
            (
                (right_hbm, right_ref),
                (dest_hbm, dest_ref),
                (choice_hbm, choice_ref),
                (psi_hbm, psi_ref),
                (left_hbm, left_ref),
            )
        )
    ]
    for load in loads:
        load.start()

    barrier = pltpu.get_barrier_semaphore()

    def greet(where):
        pl.semaphore_signal(barrier, inc=1, device_id=where, device_id_type=MESH)

    def greet_op(step, carry):
        greet({"op": op_peer(step)})
        return carry

    greet({"sec": chip(1)})
    greet({"sec": chip(-1)})
    greet({"sec": mate})
    if groups > 1:
        lax.fori_loop(1, groups, greet_op, 0)
    greetings = 3 + (groups - 1)

    def pack_right(s, carry):
        for high in range(2):
            ring[0, s, high * 64:(high + 1) * 64, :] = jnp.concatenate(
                [right_ref[2 * high, s], right_ref[2 * high + 1, s]], axis=1
            )
        return carry

    loads[0].wait()
    lax.fori_loop(0, secs, pack_right, 0)
    rows = 4 * chips
    loads[1].wait()
    loads[2].wait()
    total_secs = dest_ref.shape[1]
    width = min(128, total_secs)
    if width == 128:
        start = pl.multiple_of(lax.div(me * secs, width) * width, width)
    else:
        start = 0
    near_dest = dest_ref[:, pl.ds(start, width)]
    near_choice = choice_ref[:, pl.ds(start, width)]

    def step_of(shape):
        return lax.shift_right_logical(lax.broadcasted_iota(jnp.int32, shape, 0), 2)

    def source_of(n):
        odd = lax.rem(n, 2)
        half_n = lax.shift_right_logical(n + odd, 1)
        slot = jnp.where(odd == 1, half_n, chips - half_n)
        m = jnp.maximum(n - 2 * near, 0)
        half_m = lax.shift_right_logical(m, 1)
        slot = jnp.where(m > 0, jnp.where(lax.rem(m, 2) == 1, half + half_m, half - half_m), slot)
        return lax.rem(z - slot + 2 * chips, chips) * 2

    source = source_of(step_of((rows, width)))
    sector = lax.broadcasted_iota(jnp.int32, (1, width), 1) + start
    holder = lax.div(sector, secs)
    inside = lax.rem(sector, secs)
    count = secs * pairs
    block_l = lax.div(lax.broadcasted_iota(jnp.int32, (count, width), 0), pairs)
    block_p = lax.rem(lax.broadcasted_iota(jnp.int32, (count, width), 0), pairs)
    found = [jnp.zeros((rows, width), jnp.int32) for _ in range(4)]
    target = jnp.zeros((count, width), jnp.int32)
    for p in range(pairs):
        here = jnp.where(holder == me, near_dest[p:p + 1], -1)
        there = jnp.where(holder == mate, near_dest[p:p + 1], -1)
        pick = near_choice[p:p + 1]
        hits = (here == source + core, here == source + 1 - core, there == source + core)
        place = inside * pairs + p
        found[0] += jnp.where(hits[0], place, 0)
        found[1] += jnp.where(hits[1], place, 0)
        found[2] += jnp.where(hits[0], pick, 0)
        found[3] += jnp.where(hits[2], pick, 0)
        fits = jnp.where(block_l == inside, jnp.where(block_p == p, 1, 0), 0)
        target += fits * jnp.where(holder == me, near_dest[p:p + 1], 0)
    lane_of = lax.broadcasted_iota(jnp.int32, (rows, 128), 1)
    table = jnp.zeros((rows, 128), jnp.int32)
    for k in range(4):
        most = count - 1 if k < 2 else secs - 1
        value = jnp.minimum(jnp.sum(found[k], axis=1, keepdims=True), most)
        table += jnp.where(lane_of == k, value, 0)
    lists[0:rows, :] = table
    owner = lax.div(lax.broadcasted_iota(jnp.int32, (pairs, total_secs), 1), secs)
    for way in range(2):
        sign = 1 - 2 * way
        origin = lax.rem(z - sign * near + 2 * chips, chips) * 2 + core
        from_there = jnp.where(dest_ref[...] == origin, choice_ref[...], 0)
        for j in range(2 * FAR - 1):
            taker = lax.rem(z + sign * (j // 2 + 1) + chips, chips) * 2
            taker += core if j % 2 == (0 if j < 2 * FAR - 2 else way) else 1 - core
            wanted = jnp.where(owner == taker, from_there, 0)
            wanted = jnp.sum(jnp.sum(wanted, axis=0, keepdims=True), axis=1, keepdims=True)
            wanted = jnp.minimum(wanted, secs - 1)
            at = rows + way * (2 * FAR - 1) + j
            lists[at:at + 1, :] = jnp.broadcast_to(wanted, (1, 128))
    to_scalars = pltpu.make_async_copy(lists, tab_ref, load_sem.at[5])
    to_scalars.start()
    goal = jnp.sum(target, axis=1, keepdims=True)
    slot = lax.rem(z - lax.shift_right_logical(goal, 1) + chips, chips)
    order = jnp.where(slot < half, 2 * slot - 1, 2 * (chips - slot))
    beyond = slot - half
    order = jnp.where(
        jnp.abs(beyond) < FAR, 2 * near + jnp.where(beyond < 0, -2 * beyond, 2 * beyond + 1), order
    )
    order = jnp.where(slot == 0, 0, order)
    code = order * 2 + jnp.where(lax.rem(goal, 2) == core, 0, 1)
    code_ref[...] = jnp.broadcast_to(code, (count, 128))
    pl.semaphore_wait(barrier, greetings)

    def ring_copy(way, hop, q):
        if way == 0:
            src, dst, target = hop - 1, hop, chip(1)
        else:
            src, dst, target = lax.rem(chips + 1 - hop, chips), chips - hop, chip(-1)
        return pltpu.make_async_remote_copy(
            src_ref=ring.at[src, pl.ds(q * per, per)],
            dst_ref=ring.at[dst, pl.ds(q * per, per)],
            send_sem=ring_send.at[way, hop, q],
            recv_sem=ring_recv.at[way, hop, q],
            device_id={"sec": target},
            device_id_type=MESH,
        )

    def far_copy(way, j):
        step = j // 2 + 1
        other = j % 2 if j < 2 * FAR - 2 else way
        slot = near + step if way == 0 else chips - near - step
        taker = lax.rem(z + (1 - 2 * way) * step + chips, chips) * 2
        return pltpu.make_async_remote_copy(
            src_ref=far.at[way, j],
            dst_ref=blk.at[other * chips + slot],
            send_sem=far_send.at[way, j],
            recv_sem=pair_recv.at[slot] if other else far_recv.at[slot],
            device_id={"sec": taker + (1 - core if other else core)},
            device_id_type=MESH,
        )

    def far_arrived(slot):
        pltpu.make_async_remote_copy(
            src_ref=far.at[0, 0],
            dst_ref=blk.at[slot],
            send_sem=far_send.at[0, 0],
            recv_sem=far_recv.at[slot],
            device_id={"sec": mate},
            device_id_type=MESH,
        ).wait_recv()

    for q in range(CHUNKS):
        ring_copy(0, 1, q).start()
        ring_copy(1, 1, q).start()

    def pair_copy(slot):
        return pltpu.make_async_remote_copy(
            src_ref=pass_on.at[slot],
            dst_ref=blk.at[chips + slot],
            send_sem=pair_send.at[slot],
            recv_sem=pair_recv.at[slot],
            device_id={"sec": mate},
            device_id_type=MESH,
        )

    def shelve(slot):
        for s in range(secs):
            shelf[s] = ring[slot, s]

    def choose(slot, n):
        pass_on[slot] = shelf[tab_ref[4 * n, 3]]
        pair_copy(slot).start()
        blk[slot] = shelf[tab_ref[4 * n, 2]]

    def choose_far(way):
        takers = 2 * FAR - 1
        for j in reversed(range(takers)):
            far[way, j] = shelf[tab_ref[rows + way * takers + j, 0]]
            far_copy(way, j).start()

    to_scalars.wait()

    shelve(0)
    choose(0, 0)

    low = lax.broadcasted_iota(jnp.int32, (pairs, 128), 1) < 64

    def widen(step, carry):
        v = lax.div(step, secs)
        l = lax.rem(step, secs)
        for t in range(cells // 128):
            x = psi_ref[v, l, :, t * 128:(t + 1) * 128].astype(F32)
            r = pltpu.roll(x, 64, 1)
            wide[v, pl.ds(l * (pairs * 64) + 2 * t, pairs, stride=64), :] = jnp.where(low, x, r)
            wide[v, pl.ds(l * (pairs * 64) + 2 * t + 1, pairs, stride=64), :] = jnp.where(low, r, x)
        return carry

    loads[3].wait()
    lax.fori_loop(0, vectors * secs, widen, 0)

    def pack_left(l, carry):
        for high in range(2):
            lefts[l, high * 64:(high + 1) * 64, :] = jnp.concatenate(
                [left_ref[2 * high, l], left_ref[2 * high + 1, l]], axis=1
            )
        return carry

    loads[4].wait()
    lax.fori_loop(0, secs, pack_left, 0)
    acc[...] = jnp.zeros_like(acc)
    low64 = lax.broadcasted_iota(jnp.int32, (64, 128), 1) < 64

    def rows_of(v, place):
        return wide[v, pl.ds(place * 64, 64), :]

    def pair(slot, n):
        found = []
        tiles = []
        for w in range(2):
            place = tab_ref[4 * n, w]
            l = lax.div(place, pairs)
            mat = blk[w * chips + slot]
            ys = [rows_of(v, place) for v in range(vectors)]
            tiles.append(ys)
            lhs = jnp.concatenate(
                [jnp.where(low64, y, 0.0).astype(BF16) for y in ys]
                + [jnp.where(low64, 0.0, y).astype(BF16) for y in ys], axis=0
            )
            inner = lax.dot_general(
                lhs, mat, (((1,), (1,)), ((), ())), preferred_element_type=F32
            ).astype(BF16)
            rhs = jnp.concatenate(
                [
                    jnp.concatenate(
                        [inner[v * 64:(v + 1) * 64], inner[(vectors + v) * 64:(vectors + v + 1) * 64]],
                        axis=0,
                    )
                    for v in range(vectors)
                ],
                axis=1,
            )
            out = jnp.dot(lefts[l], rhs, preferred_element_type=F32)
            sums = []
            for v in range(vectors):
                top = out[0:64, v * 128:(v + 1) * 128]
                bottom = out[64:128, v * 128:(v + 1) * 128]
                if w == 0:
                    sums.append(top + pltpu.roll(bottom, 64, 1))
                else:
                    sums.append(pltpu.roll(top, 64, 1) + bottom)
            found.append(sums)
        parts = []
        for v in range(vectors):
            part = jnp.where(low64, found[0][v], found[1][v]).astype(BF16).astype(F32)
            stage[lax.rem(n, 4), v] = part
            parts.append(part)
        for v in range(vectors):
            both = jnp.where(low64, tiles[0][v], tiles[1][v])
            for w in range(vectors):
                prod = (both * parts[w]).reshape(8, 8, 128)
                acc[v * vectors + w] += jnp.sum(prod, axis=0)

    low4 = lax.broadcasted_iota(jnp.int32, (8, 8, 128), 1) < 4

    def op_copy(step, batch):
        peer = op_peer(step)
        return pltpu.make_async_remote_copy(
            src_ref=outbox.at[batch, peer],
            dst_ref=inbox.at[batch, op],
            send_sem=op_send.at[batch],
            recv_sem=op_recv.at[batch],
            device_id={"op": peer},
            device_id_type=MESH,
        )

    def finish(batch):
        for v in range(vectors):
            xs = [stage[j, v].reshape(8, 8, 128) for j in range(4)]
            ev, od = [], []
            for j in (0, 2):
                x, y = xs[j], xs[j + 1]
                ev.append(jnp.where(low4, x, pltpu.roll(y, 4, 1)))
                od.append(jnp.where(low4, pltpu.roll(x, 4, 1), y))
            even = jnp.concatenate(ev, axis=1).astype(BF16)
            odd = jnp.concatenate(od, axis=1).astype(BF16)
            for t in range(8):
                outbox[batch, 2 * t, v * 16:(v + 1) * 16, :] = even[t]
                outbox[batch, 2 * t + 1, v * 16:(v + 1) * 16, :] = odd[t]
        if groups > 1:

            def send(step, carry):
                op_copy(step, batch).start()
                return carry

            lax.fori_loop(1, groups, send, 0)
        inbox[batch, op] = outbox[batch, op]

    def gather_sum(batch):
        if groups > 1:
            pltpu.make_async_remote_copy(
                src_ref=outbox.at[batch, pl.ds(0, groups - 1)],
                dst_ref=inbox.at[batch, pl.ds(0, groups - 1)],
                send_sem=op_send.at[batch],
                recv_sem=op_recv.at[batch],
                device_id={"op": op_peer(1)},
                device_id_type=MESH,
            ).wait()
        value = inbox[batch, 0].astype(F32)
        for g in range(1, groups):
            value += inbox[batch, g].astype(F32)
        total[batch] = value.astype(BF16)

    def first_pair(h):
        pair_copy(h - 1).wait_recv()
        pair(h - 1, 2 * (h - 1) - 1 + lax.div(half - h, half - 1))

        @pl.when(jnp.logical_and(lax.rem(h, 2) == 1, h >= 3))
        def _():
            finish(lax.div(h - 3, 2))

    def second_pair(h):
        @pl.when(h >= 2)
        def _():
            pair_copy(chips - (h - 1)).wait_recv()
            pair(chips - (h - 1), 2 * (h - 1))

        @pl.when(jnp.logical_and(lax.rem(h, 2) == 1, h >= 5))
        def _():
            gather_sum(lax.div(h - 5, 2))

    def turn(h, carry):
        def serve(q):
            for way in range(2):
                ring_copy(way, h, q).wait_recv()

                @pl.when(h < near)
                def _():
                    ring_copy(way, h + 1, q).start()

        for q in range(CHUNKS // 2):
            serve(q)
        first_pair(h)
        for q in range(CHUNKS // 2, CHUNKS):
            serve(q)
        for way in range(2):
            slot = h if way == 0 else chips - h
            shelve(slot)

            @pl.when(h == near)
            def _():
                choose_far(way)

            choose(slot, 2 * h - 1 + way)
        second_pair(h)
        return carry

    lax.fori_loop(1, near + 1, turn, 0)

    def pairs_of(h, carry):
        first_pair(h)
        second_pair(h)
        return carry

    lax.fori_loop(near + 1, near + 2, pairs_of, 0)

    def far_turn(m, carry):
        half_m = lax.div(m, 2)
        slot = half + (2 * lax.rem(m, 2) - 1) * half_m
        n = 2 * near + m
        pair_copy(slot).wait_recv()
        far_arrived(slot)
        pair(slot, n)

        @pl.when(jnp.logical_and(lax.rem(n, 4) == 3, n < chips - 1))
        def _():
            finish(lax.div(n, 4))

        return carry

    lax.fori_loop(1, 2 * FAR, far_turn, 0)

    lane = lax.broadcasted_iota(jnp.int32, (1, 128), 1)
    row = jnp.zeros((1, 128), F32)
    for i in range(vectors * vectors):
        whole = jnp.sum(jnp.sum(acc[i], axis=0, keepdims=True), axis=1, keepdims=True)
        row += jnp.where(lane == i, whole, 0.0)
    dots[...] = row
    if groups > 1:

        def dot_copy(step):
            return pltpu.make_async_remote_copy(
                src_ref=dots,
                dst_ref=dots_op.at[op],
                send_sem=dot_send.at[0],
                recv_sem=dot_recv.at[0],
                device_id={"op": op_peer(step)},
                device_id_type=MESH,
            )

        def send_dots(step, carry):
            dot_copy(step).start()
            return carry

        lax.fori_loop(1, groups, send_dots, 0)
    dots_op[op] = dots[...]
    finish(batches - 1)

    if groups > 1:
        pltpu.make_async_remote_copy(
            src_ref=dots_op.at[pl.ds(0, groups - 1)],
            dst_ref=dots_op.at[pl.ds(0, groups - 1)],
            send_sem=dot_send.at[0],
            recv_sem=dot_recv.at[0],
            device_id={"op": op_peer(1)},
            device_id_type=MESH,
        ).wait()
    value = dots_op[0]
    for g in range(1, groups):
        value += dots_op[g]
    one[...] = value
    core_copy = pltpu.make_async_remote_copy(
        src_ref=one,
        dst_ref=dots_core,
        send_sem=dot_send.at[1],
        recv_sem=dot_recv.at[1],
        device_id={"sec": mate},
        device_id_type=MESH,
    )
    core_copy.start()
    for batch in range(max(0, (near - 4) // 2 + 1), batches - 1):
        gather_sum(batch)
    core_copy.wait()
    two[...] = one[...] + dots_core[...]

    def send_chip(step, carry):
        pltpu.make_async_remote_copy(
            src_ref=two,
            dst_ref=dots_chip.at[z],
            send_sem=dot_send.at[2],
            recv_sem=dot_recv.at[2],
            device_id={"sec": chip(step)},
            device_id_type=MESH,
        ).start()
        return carry

    def send_chips(step, carry):
        send_chip(half - step, 0)
        send_chip(half + step, 0)
        return carry

    send_chip(half, 0)
    lax.fori_loop(1, half, send_chips, 0)
    dots_chip[z] = two[...]
    gather_sum(batches - 1)

    code = code_ref[...]
    second = lax.rem(code, 2) == 1
    base = lax.div(code, 2) * 4
    column = lax.broadcasted_iota(jnp.int32, (64, 128), 1)
    for v in range(vectors):
        table = total[:, v * 16:(v + 1) * 16, :].reshape(rows, 128)
        got = []
        for i in range(4):
            hot = jnp.where(column[:count, :rows] == base[:, :rows] + i, 1.0, 0.0).astype(BF16)
            got.append(jnp.dot(hot, table, preferred_element_type=F32))
        lanes = column[:count] < 64
        for i in range(2):
            x = jnp.where(second, pltpu.roll(got[2 * i], 64, 1), got[2 * i])
            y = jnp.where(second, got[2 * i + 1], pltpu.roll(got[2 * i + 1], 64, 1))
            sig_ref[v, :, i * 128:(i + 1) * 128] = jnp.where(lanes, x, y).astype(BF16)

    def drain(h, carry):
        for q in range(CHUNKS):
            for way in range(2):
                ring_copy(way, h, q).wait_send()
        return carry

    lax.fori_loop(1, near + 1, drain, 0)

    for way in range(2):
        for j in range(2 * FAR - 1):
            far_copy(way, j).wait_send()

    def drain_pairs(slot, carry):
        pair_copy(slot).wait_send()
        return carry

    lax.fori_loop(0, near + 1, drain_pairs, 0)
    lax.fori_loop(chips - near, chips, drain_pairs, 0)

    pltpu.make_async_remote_copy(
        src_ref=dots_chip.at[pl.ds(0, chips - 1)],
        dst_ref=dots_chip.at[pl.ds(0, chips - 1)],
        send_sem=dot_send.at[2],
        recv_sem=dot_recv.at[2],
        device_id={"sec": chip(1)},
        device_id_type=MESH,
    ).wait()
    value = dots_chip[0]
    for g in range(1, chips):
        value += dots_chip[g]
    value = value * scale
    for v in range(vectors):
        for w in range(vectors):
            i = v * vectors + w
            sub_ref[v:v + 1, w:w + 1] = value[:, i:i + 1]


def body(psi, left_ops, right_ops, dest_dev, right_sub):
    vectors, secs, pairs, cells = psi.shape
    terms = left_ops.shape[0]
    devices = lax.axis_size("sec")
    groups = lax.axis_size("op")
    chips = devices // 2
    count = secs * pairs
    half = chips // 2
    entries = secs * devices * pairs * cells
    batches = chips // 4
    vmem = pltpu.VMEM
    dma = pltpu.SemaphoreType.DMA
    sigma, subspace = pl.pallas_call(
        functools.partial(kernel, chips, groups, 1.0 / entries),
        out_shape=(
            jax.ShapeDtypeStruct((vectors, count, cells // 16), BF16),
            jax.ShapeDtypeStruct((vectors, vectors), F32),
        ),
        in_specs=[pl.BlockSpec(memory_space=pl.ANY)] * 5,
        out_specs=(pl.BlockSpec(memory_space=pltpu.VMEM), pl.BlockSpec(memory_space=pltpu.VMEM)),
        scratch_shapes=[
            vmem(psi.shape, BF16),
            vmem(left_ops.shape, BF16),
            vmem(right_ops.shape, BF16),
            vmem((pairs, secs * devices), jnp.int32),
            vmem((pairs, secs * devices), jnp.int32),
            vmem((4 * chips + 16, 128), jnp.int32),
            pltpu.SMEM((4 * chips + 16, 128), jnp.int32),
            vmem((count, 128), jnp.int32),
            vmem((chips, secs, 128, 128), BF16),
            vmem((2, 2 * FAR - 1, 128, 128), BF16),
            vmem((2 * chips, 128, 128), BF16),
            vmem((chips, 128, 128), BF16),
            vmem((vectors, count * 64, 128), F32),
            vmem((secs, 128, 128), BF16),
            vmem((4, vectors, 64, 128), F32),
            vmem((batches, 16, vectors * 16, 128), BF16),
            vmem((batches, groups, vectors * 16, 128), BF16),
            vmem((batches, vectors * 16, 128), BF16),
            vmem((vectors * vectors, 8, 128), F32),
            vmem((1, 128), F32),
            vmem((groups, 1, 128), F32),
            vmem((1, 128), F32),
            vmem((chips, 1, 128), F32),
            vmem((1, 128), F32),
            vmem((1, 128), F32),
            vmem((secs, 128, 128), BF16),
            dma((6,)),
            dma((2, half + 1, CHUNKS)),
            dma((2, half + 1, CHUNKS)),
            dma((2, 2 * FAR - 1)),
            dma((chips,)),
            dma((chips,)),
            dma((chips,)),
            dma((batches,)),
            dma((batches,)),
            dma((3,)),
            dma((3,)),
        ],
        compiler_params=pltpu.CompilerParams(
            collective_id=0, has_side_effects=True, vmem_limit_bytes=56 * 1024 * 1024
        ),
        cost_estimate=pl.CostEstimate(
            flops=4 * terms * vectors * count * 64 ** 3, bytes_accessed=8 << 20, transcendentals=0
        ),
    )(psi, left_ops, right_ops, dest_dev.T, right_sub.T)
    return sigma.reshape(vectors, secs, pairs, cells // 16), subspace


def solution(mesh):
    return jax.shard_map(
        body,
        mesh=mesh,
        in_specs=(
            P(None, "sec", None, None),
            P("op", "sec", None, None),
            P("op", "sec", None, None),
            P(),
            P(),
        ),
        out_specs=(P(None, "sec", None, "op"), P()),
        check_vma=False,
    )
```

```python
import functools

import jax
import jax.numpy as jnp
from jax import lax
from jax.experimental import pallas as pl
from jax.experimental.pallas import tpu as pltpu
from jax.sharding import PartitionSpec as P

MESH = pl.DeviceIdType.MESH
CHUNKS = 2
FAR = 4
F32 = jnp.float32
BF16 = jnp.bfloat16


def kernel(
    chips, groups, scale,
    psi_hbm, left_hbm, right_hbm, dest_hbm, choice_hbm,
    sig_ref, sub_ref,
    psi_ref, left_ref, right_ref, dest_ref, choice_ref, lists, tab_ref, code_ref, ring, far, blk, pass_on, wide, lefts, stage, outbox, inbox, total, acc,
    dots, dots_op, dots_core, dots_chip, one, two, shelf,
    load_sem, ring_send, ring_recv, far_send, far_recv, pair_send, pair_recv, op_send, op_recv, dot_send, dot_recv,
):
    half = chips // 2
    near = half - FAR
    vectors, secs, pairs, cells = psi_ref.shape
    batches = chips // 4
    per = secs // CHUNKS
    me = lax.axis_index("sec")
    core = lax.rem(me, 2)
    z = lax.div(me, 2)
    op = lax.axis_index("op")
    mate = z * 2 + 1 - core

    def chip(step):
        return lax.rem(z + step + chips, chips) * 2 + core

    def op_peer(step):
        return lax.rem(op + step, groups)

    loads = [
        pltpu.make_async_copy(src, dst, load_sem.at[i])
        for i, (src, dst) in enumerate(
            (
                (right_hbm, right_ref),
                (dest_hbm, dest_ref),
                (choice_hbm, choice_ref),
                (psi_hbm, psi_ref),
                (left_hbm, left_ref),
            )
        )
    ]
    for load in loads:
        load.start()

    barrier = pltpu.get_barrier_semaphore()

    def greet(where):
        pl.semaphore_signal(barrier, inc=1, device_id=where, device_id_type=MESH)

    def greet_op(step, carry):
        greet({"op": op_peer(step)})
        return carry

    greet({"sec": chip(1)})
    greet({"sec": chip(-1)})
    greet({"sec": mate})
    if groups > 1:
        lax.fori_loop(1, groups, greet_op, 0)
    greetings = 3 + (groups - 1)

    def pack_right(s, carry):
        for high in range(2):
            ring[0, s, high * 64:(high + 1) * 64, :] = jnp.concatenate(
                [right_ref[2 * high, s], right_ref[2 * high + 1, s]], axis=1
            )
        return carry

    loads[0].wait()
    lax.fori_loop(0, secs, pack_right, 0)
    rows = 4 * chips
    loads[1].wait()
    loads[2].wait()
    total_secs = dest_ref.shape[1]
    width = min(128, total_secs)
    if width == 128:
        start = pl.multiple_of(lax.div(me * secs, width) * width, width)
    else:
        start = 0
    near_dest = dest_ref[:, pl.ds(start, width)]
    near_choice = choice_ref[:, pl.ds(start, width)]

    def step_of(shape):
        return lax.shift_right_logical(lax.broadcasted_iota(jnp.int32, shape, 0), 2)

    def source_of(n):
        odd = lax.rem(n, 2)
        half_n = lax.shift_right_logical(n + odd, 1)
        slot = jnp.where(odd == 1, half_n, chips - half_n)
        m = jnp.maximum(n - 2 * near, 0)
        half_m = lax.shift_right_logical(m, 1)
        slot = jnp.where(m > 0, jnp.where(lax.rem(m, 2) == 1, half + half_m, half - half_m), slot)
        return lax.rem(z - slot + 2 * chips, chips) * 2

    source = source_of(step_of((rows, width)))
    sector = lax.broadcasted_iota(jnp.int32, (1, width), 1) + start
    holder = lax.div(sector, secs)
    inside = lax.rem(sector, secs)
    count = secs * pairs
    block_l = lax.div(lax.broadcasted_iota(jnp.int32, (count, width), 0), pairs)
    block_p = lax.rem(lax.broadcasted_iota(jnp.int32, (count, width), 0), pairs)
    found = [jnp.zeros((rows, width), jnp.int32) for _ in range(4)]
    target = jnp.zeros((count, width), jnp.int32)
    for p in range(pairs):
        here = jnp.where(holder == me, near_dest[p:p + 1], -1)
        there = jnp.where(holder == mate, near_dest[p:p + 1], -1)
        pick = near_choice[p:p + 1]
        hits = (here == source + core, here == source + 1 - core, there == source + core)
        place = inside * pairs + p
        found[0] += jnp.where(hits[0], place, 0)
        found[1] += jnp.where(hits[1], place, 0)
        found[2] += jnp.where(hits[0], pick, 0)
        found[3] += jnp.where(hits[2], pick, 0)
        fits = jnp.where(block_l == inside, jnp.where(block_p == p, 1, 0), 0)
        target += fits * jnp.where(holder == me, near_dest[p:p + 1], 0)
    lane_of = lax.broadcasted_iota(jnp.int32, (rows, 128), 1)
    table = jnp.zeros((rows, 128), jnp.int32)
    for k in range(4):
        most = count - 1 if k < 2 else secs - 1
        value = jnp.minimum(jnp.sum(found[k], axis=1, keepdims=True), most)
        table += jnp.where(lane_of == k, value, 0)
    lists[0:rows, :] = table
    owner = lax.div(lax.broadcasted_iota(jnp.int32, (pairs, total_secs), 1), secs)
    for way in range(2):
        sign = 1 - 2 * way
        origin = lax.rem(z - sign * near + 2 * chips, chips) * 2 + core
        from_there = jnp.where(dest_ref[...] == origin, choice_ref[...], 0)
        for j in range(2 * FAR - 1):
            taker = lax.rem(z + sign * (j // 2 + 1) + chips, chips) * 2
            taker += core if j % 2 == (0 if j < 2 * FAR - 2 else way) else 1 - core
            wanted = jnp.where(owner == taker, from_there, 0)
            wanted = jnp.sum(jnp.sum(wanted, axis=0, keepdims=True), axis=1, keepdims=True)
            wanted = jnp.minimum(wanted, secs - 1)
            at = rows + way * (2 * FAR - 1) + j
            lists[at:at + 1, :] = jnp.broadcast_to(wanted, (1, 128))
    to_scalars = pltpu.make_async_copy(lists, tab_ref, load_sem.at[5])
    to_scalars.start()
    goal = jnp.sum(target, axis=1, keepdims=True)
    slot = lax.rem(z - lax.shift_right_logical(goal, 1) + chips, chips)
    order = jnp.where(slot < half, 2 * slot - 1, 2 * (chips - slot))
    beyond = slot - half
    order = jnp.where(
        jnp.abs(beyond) < FAR, 2 * near + jnp.where(beyond < 0, -2 * beyond, 2 * beyond + 1), order
    )
    order = jnp.where(slot == 0, 0, order)
    code = order * 2 + jnp.where(lax.rem(goal, 2) == core, 0, 1)
    code_ref[...] = jnp.broadcast_to(code, (count, 128))
    pl.semaphore_wait(barrier, greetings)

    def ring_copy(way, hop, q):
        if way == 0:
            src, dst, target = hop - 1, hop, chip(1)
        else:
            src, dst, target = lax.rem(chips + 1 - hop, chips), chips - hop, chip(-1)
        return pltpu.make_async_remote_copy(
            src_ref=ring.at[src, pl.ds(q * per, per)],
            dst_ref=ring.at[dst, pl.ds(q * per, per)],
            send_sem=ring_send.at[way, hop, q],
            recv_sem=ring_recv.at[way, hop, q],
            device_id={"sec": target},
            device_id_type=MESH,
        )

    def far_copy(way, j):
        step = j // 2 + 1
        other = j % 2 if j < 2 * FAR - 2 else way
        slot = near + step if way == 0 else chips - near - step
        taker = lax.rem(z + (1 - 2 * way) * step + chips, chips) * 2
        return pltpu.make_async_remote_copy(
            src_ref=far.at[way, j],
            dst_ref=blk.at[other * chips + slot],
            send_sem=far_send.at[way, j],
            recv_sem=pair_recv.at[slot] if other else far_recv.at[slot],
            device_id={"sec": taker + (1 - core if other else core)},
            device_id_type=MESH,
        )

    def far_arrived(slot):
        pltpu.make_async_remote_copy(
            src_ref=far.at[0, 0],
            dst_ref=blk.at[slot],
            send_sem=far_send.at[0, 0],
            recv_sem=far_recv.at[slot],
            device_id={"sec": mate},
            device_id_type=MESH,
        ).wait_recv()

    for q in range(CHUNKS):
        ring_copy(0, 1, q).start()
        ring_copy(1, 1, q).start()

    def pair_copy(slot):
        return pltpu.make_async_remote_copy(
            src_ref=pass_on.at[slot],
            dst_ref=blk.at[chips + slot],
            send_sem=pair_send.at[slot],
            recv_sem=pair_recv.at[slot],
            device_id={"sec": mate},
            device_id_type=MESH,
        )

    def shelve(slot, at):
        for s in range(secs):
            shelf[at, s] = ring[slot, s]

    def choose(slot, n, at):
        pass_on[slot] = shelf[at, tab_ref[4 * n, 3]]
        pair_copy(slot).start()
        blk[slot] = shelf[at, tab_ref[4 * n, 2]]

    def choose_far(way):
        takers = 2 * FAR - 1
        for j in reversed(range(takers)):
            far[way, j] = shelf[way, tab_ref[rows + way * takers + j, 0]]
            far_copy(way, j).start()

    to_scalars.wait()

    shelve(0, 0)
    choose(0, 0, 0)

    low = lax.broadcasted_iota(jnp.int32, (pairs, 128), 1) < 64

    def widen(step, carry):
        v = lax.div(step, secs)
        l = lax.rem(step, secs)
        for t in range(cells // 128):
            x = psi_ref[v, l, :, t * 128:(t + 1) * 128].astype(F32)
            r = pltpu.roll(x, 64, 1)
            wide[v, pl.ds(l * (pairs * 64) + 2 * t, pairs, stride=64), :] = jnp.where(low, x, r)
            wide[v, pl.ds(l * (pairs * 64) + 2 * t + 1, pairs, stride=64), :] = jnp.where(low, r, x)
        return carry

    loads[3].wait()
    lax.fori_loop(0, vectors * secs, widen, 0)

    def pack_left(l, carry):
        for high in range(2):
            lefts[l, high * 64:(high + 1) * 64, :] = jnp.concatenate(
                [left_ref[2 * high, l], left_ref[2 * high + 1, l]], axis=1
            )
        return carry

    loads[4].wait()
    lax.fori_loop(0, secs, pack_left, 0)
    acc[...] = jnp.zeros_like(acc)
    low64 = lax.broadcasted_iota(jnp.int32, (64, 128), 1) < 64

    def rows_of(v, place):
        return wide[v, pl.ds(place * 64, 64), :]

    def pair(slot, n):
        found = []
        tiles = []
        for w in range(2):
            place = tab_ref[4 * n, w]
            l = lax.div(place, pairs)
            mat = blk[w * chips + slot]
            ys = [rows_of(v, place) for v in range(vectors)]
            tiles.append(ys)
            lhs = jnp.concatenate(
                [jnp.where(low64, y, 0.0).astype(BF16) for y in ys]
                + [jnp.where(low64, 0.0, y).astype(BF16) for y in ys], axis=0
            )
            inner = lax.dot_general(
                lhs, mat, (((1,), (1,)), ((), ())), preferred_element_type=F32
            ).astype(BF16)
            rhs = jnp.concatenate(
                [
                    jnp.concatenate(
                        [inner[v * 64:(v + 1) * 64], inner[(vectors + v) * 64:(vectors + v + 1) * 64]],
                        axis=0,
                    )
                    for v in range(vectors)
                ],
                axis=1,
            )
            out = jnp.dot(lefts[l], rhs, preferred_element_type=F32)
            sums = []
            for v in range(vectors):
                top = out[0:64, v * 128:(v + 1) * 128]
                bottom = out[64:128, v * 128:(v + 1) * 128]
                if w == 0:
                    sums.append(top + pltpu.roll(bottom, 64, 1))
                else:
                    sums.append(pltpu.roll(top, 64, 1) + bottom)
            found.append(sums)
        parts = []
        for v in range(vectors):
            part = jnp.where(low64, found[0][v], found[1][v]).astype(BF16).astype(F32)
            stage[lax.rem(n, 4), v] = part
            parts.append(part)
        for v in range(vectors):
            both = jnp.where(low64, tiles[0][v], tiles[1][v])
            for w in range(vectors):
                prod = (both * parts[w]).reshape(8, 8, 128)
                acc[v * vectors + w] += jnp.sum(prod, axis=0)

    low4 = lax.broadcasted_iota(jnp.int32, (8, 8, 128), 1) < 4

    def op_copy(step, batch):
        peer = op_peer(step)
        return pltpu.make_async_remote_copy(
            src_ref=outbox.at[batch, peer],
            dst_ref=inbox.at[batch, op],
            send_sem=op_send.at[batch],
            recv_sem=op_recv.at[batch],
            device_id={"op": peer},
            device_id_type=MESH,
        )

    def finish(batch):
        for v in range(vectors):
            xs = [stage[j, v].reshape(8, 8, 128) for j in range(4)]
            ev, od = [], []
            for j in (0, 2):
                x, y = xs[j], xs[j + 1]
                ev.append(jnp.where(low4, x, pltpu.roll(y, 4, 1)))
                od.append(jnp.where(low4, pltpu.roll(x, 4, 1), y))
            even = jnp.concatenate(ev, axis=1).astype(BF16)
            odd = jnp.concatenate(od, axis=1).astype(BF16)
            for t in range(8):
                outbox[batch, 2 * t, v * 16:(v + 1) * 16, :] = even[t]
                outbox[batch, 2 * t + 1, v * 16:(v + 1) * 16, :] = odd[t]
        if groups > 1:

            def send(step, carry):
                op_copy(step, batch).start()
                return carry

            lax.fori_loop(1, groups, send, 0)
        inbox[batch, op] = outbox[batch, op]

    def gather_sum(batch):
        if groups > 1:
            pltpu.make_async_remote_copy(
                src_ref=outbox.at[batch, pl.ds(0, groups - 1)],
                dst_ref=inbox.at[batch, pl.ds(0, groups - 1)],
                send_sem=op_send.at[batch],
                recv_sem=op_recv.at[batch],
                device_id={"op": op_peer(1)},
                device_id_type=MESH,
            ).wait()
        value = inbox[batch, 0].astype(F32)
        for g in range(1, groups):
            value += inbox[batch, g].astype(F32)
        total[batch] = value.astype(BF16)

    def first_pair(h):
        pair_copy(h - 1).wait_recv()
        pair(h - 1, 2 * (h - 1) - 1 + lax.div(half - h, half - 1))

        @pl.when(jnp.logical_and(lax.rem(h, 2) == 1, h >= 3))
        def _():
            finish(lax.div(h - 3, 2))

    def second_pair(h):
        @pl.when(h >= 2)
        def _():
            pair_copy(chips - (h - 1)).wait_recv()
            pair(chips - (h - 1), 2 * (h - 1))

        @pl.when(jnp.logical_and(lax.rem(h, 2) == 1, h >= 5))
        def _():
            gather_sum(lax.div(h - 5, 2))

    def turn(h, carry):
        def serve(q):
            for way in range(2):
                ring_copy(way, h, q).wait_recv()

                @pl.when(h < near)
                def _():
                    ring_copy(way, h + 1, q).start()

        for q in range(CHUNKS // 2):
            serve(q)
        first_pair(h)
        for q in range(CHUNKS // 2, CHUNKS):
            serve(q)
        for way in range(2):
            slot = h if way == 0 else chips - h
            shelve(slot, way)

            @pl.when(h == near)
            def _():
                choose_far(way)

        for way in range(2):
            choose(h if way == 0 else chips - h, 2 * h - 1 + way, way)
        second_pair(h)
        return carry

    lax.fori_loop(1, near + 1, turn, 0)

    def pairs_of(h, carry):
        first_pair(h)
        second_pair(h)
        return carry

    lax.fori_loop(near + 1, near + 2, pairs_of, 0)

    def far_turn(m, carry):
        half_m = lax.div(m, 2)
        slot = half + (2 * lax.rem(m, 2) - 1) * half_m
        n = 2 * near + m
        pair_copy(slot).wait_recv()
        far_arrived(slot)
        pair(slot, n)

        @pl.when(jnp.logical_and(lax.rem(n, 4) == 3, n < chips - 1))
        def _():
            finish(lax.div(n, 4))

        return carry

    lax.fori_loop(1, 2 * FAR, far_turn, 0)

    lane = lax.broadcasted_iota(jnp.int32, (1, 128), 1)
    row = jnp.zeros((1, 128), F32)
    for i in range(vectors * vectors):
        whole = jnp.sum(jnp.sum(acc[i], axis=0, keepdims=True), axis=1, keepdims=True)
        row += jnp.where(lane == i, whole, 0.0)
    dots[...] = row
    if groups > 1:

        def dot_copy(step):
            return pltpu.make_async_remote_copy(
                src_ref=dots,
                dst_ref=dots_op.at[op],
                send_sem=dot_send.at[0],
                recv_sem=dot_recv.at[0],
                device_id={"op": op_peer(step)},
                device_id_type=MESH,
            )

        def send_dots(step, carry):
            dot_copy(step).start()
            return carry

        lax.fori_loop(1, groups, send_dots, 0)
    dots_op[op] = dots[...]
    finish(batches - 1)

    if groups > 1:
        pltpu.make_async_remote_copy(
            src_ref=dots_op.at[pl.ds(0, groups - 1)],
            dst_ref=dots_op.at[pl.ds(0, groups - 1)],
            send_sem=dot_send.at[0],
            recv_sem=dot_recv.at[0],
            device_id={"op": op_peer(1)},
            device_id_type=MESH,
        ).wait()
    value = dots_op[0]
    for g in range(1, groups):
        value += dots_op[g]
    one[...] = value
    core_copy = pltpu.make_async_remote_copy(
        src_ref=one,
        dst_ref=dots_core,
        send_sem=dot_send.at[1],
        recv_sem=dot_recv.at[1],
        device_id={"sec": mate},
        device_id_type=MESH,
    )
    core_copy.start()
    for batch in range(max(0, (near - 4) // 2 + 1), batches - 1):
        gather_sum(batch)
    core_copy.wait()
    two[...] = one[...] + dots_core[...]

    def send_chip(step, carry):
        pltpu.make_async_remote_copy(
            src_ref=two,
            dst_ref=dots_chip.at[z],
            send_sem=dot_send.at[2],
            recv_sem=dot_recv.at[2],
            device_id={"sec": chip(step)},
            device_id_type=MESH,
        ).start()
        return carry

    def send_chips(step, carry):
        send_chip(half - step, 0)
        send_chip(half + step, 0)
        return carry

    send_chip(half, 0)
    lax.fori_loop(1, half, send_chips, 0)
    dots_chip[z] = two[...]
    gather_sum(batches - 1)

    code = code_ref[...]
    second = lax.rem(code, 2) == 1
    base = lax.div(code, 2) * 4
    column = lax.broadcasted_iota(jnp.int32, (64, 128), 1)
    for v in range(vectors):
        table = total[:, v * 16:(v + 1) * 16, :].reshape(rows, 128)
        got = []
        for i in range(4):
            hot = jnp.where(column[:count, :rows] == base[:, :rows] + i, 1.0, 0.0).astype(BF16)
            got.append(jnp.dot(hot, table, preferred_element_type=F32))
        lanes = column[:count] < 64
        for i in range(2):
            x = jnp.where(second, pltpu.roll(got[2 * i], 64, 1), got[2 * i])
            y = jnp.where(second, got[2 * i + 1], pltpu.roll(got[2 * i + 1], 64, 1))
            sig_ref[v, :, i * 128:(i + 1) * 128] = jnp.where(lanes, x, y).astype(BF16)

    def drain(h, carry):
        for q in range(CHUNKS):
            for way in range(2):
                ring_copy(way, h, q).wait_send()
        return carry

    lax.fori_loop(1, near + 1, drain, 0)

    for way in range(2):
        for j in range(2 * FAR - 1):
            far_copy(way, j).wait_send()

    def drain_pairs(slot, carry):
        pair_copy(slot).wait_send()
        return carry

    lax.fori_loop(0, near + 1, drain_pairs, 0)
    lax.fori_loop(chips - near, chips, drain_pairs, 0)

    pltpu.make_async_remote_copy(
        src_ref=dots_chip.at[pl.ds(0, chips - 1)],
        dst_ref=dots_chip.at[pl.ds(0, chips - 1)],
        send_sem=dot_send.at[2],
        recv_sem=dot_recv.at[2],
        device_id={"sec": chip(1)},
        device_id_type=MESH,
    ).wait()
    value = dots_chip[0]
    for g in range(1, chips):
        value += dots_chip[g]
    value = value * scale
    for v in range(vectors):
        for w in range(vectors):
            i = v * vectors + w
            sub_ref[v:v + 1, w:w + 1] = value[:, i:i + 1]


def body(psi, left_ops, right_ops, dest_dev, right_sub):
    vectors, secs, pairs, cells = psi.shape
    terms = left_ops.shape[0]
    devices = lax.axis_size("sec")
    groups = lax.axis_size("op")
    chips = devices // 2
    count = secs * pairs
    half = chips // 2
    entries = secs * devices * pairs * cells
    batches = chips // 4
    vmem = pltpu.VMEM
    dma = pltpu.SemaphoreType.DMA
    sigma, subspace = pl.pallas_call(
        functools.partial(kernel, chips, groups, 1.0 / entries),
        out_shape=(
            jax.ShapeDtypeStruct((vectors, count, cells // 16), BF16),
            jax.ShapeDtypeStruct((vectors, vectors), F32),
        ),
        in_specs=[pl.BlockSpec(memory_space=pl.ANY)] * 5,
        out_specs=(pl.BlockSpec(memory_space=pltpu.VMEM), pl.BlockSpec(memory_space=pltpu.VMEM)),
        scratch_shapes=[
            vmem(psi.shape, BF16),
            vmem(left_ops.shape, BF16),
            vmem(right_ops.shape, BF16),
            vmem((pairs, secs * devices), jnp.int32),
            vmem((pairs, secs * devices), jnp.int32),
            vmem((4 * chips + 16, 128), jnp.int32),
            pltpu.SMEM((4 * chips + 16, 128), jnp.int32),
            vmem((count, 128), jnp.int32),
            vmem((chips, secs, 128, 128), BF16),
            vmem((2, 2 * FAR - 1, 128, 128), BF16),
            vmem((2 * chips, 128, 128), BF16),
            vmem((chips, 128, 128), BF16),
            vmem((vectors, count * 64, 128), F32),
            vmem((secs, 128, 128), BF16),
            vmem((4, vectors, 64, 128), F32),
            vmem((batches, 16, vectors * 16, 128), BF16),
            vmem((batches, groups, vectors * 16, 128), BF16),
            vmem((batches, vectors * 16, 128), BF16),
            vmem((vectors * vectors, 8, 128), F32),
            vmem((1, 128), F32),
            vmem((groups, 1, 128), F32),
            vmem((1, 128), F32),
            vmem((chips, 1, 128), F32),
            vmem((1, 128), F32),
            vmem((1, 128), F32),
            vmem((2, secs, 128, 128), BF16),
            dma((6,)),
            dma((2, half + 1, CHUNKS)),
            dma((2, half + 1, CHUNKS)),
            dma((2, 2 * FAR - 1)),
            dma((chips,)),
            dma((chips,)),
            dma((chips,)),
            dma((batches,)),
            dma((batches,)),
            dma((3,)),
            dma((3,)),
        ],
        compiler_params=pltpu.CompilerParams(
            collective_id=0, has_side_effects=True, vmem_limit_bytes=56 * 1024 * 1024
        ),
        cost_estimate=pl.CostEstimate(
            flops=4 * terms * vectors * count * 64 ** 3, bytes_accessed=8 << 20, transcendentals=0
        ),
    )(psi, left_ops, right_ops, dest_dev.T, right_sub.T)
    return sigma.reshape(vectors, secs, pairs, cells // 16), subspace


def solution(mesh):
    return jax.shard_map(
        body,
        mesh=mesh,
        in_specs=(
            P(None, "sec", None, None),
            P("op", "sec", None, None),
            P("op", "sec", None, None),
            P(),
            P(),
        ),
        out_specs=(P(None, "sec", None, "op"), P()),
        check_vma=False,
    )
```
